128 devices in a mesh: side: 2 (over y_lo), owner: 32 (over z, x, y_hi), seq: 2 (over core).
Axes of the slice: x: 4, y: 4 (y_hi: 2, y_lo: 2; y = y_hi * 2 + y_lo), z: 4, core: 2. Of those that a mesh axis runs over, the one named last changes fastest.
Arguments:
- prompt_hidden: bfloat16 [16384, 7168], P(('side', 'seq'), 'owner'), may hold values from -12 to 12
- latent_weight: bfloat16 [7168, 576], P('owner'), may hold values from -2 to 2
- kv_gain: float32 [512], replicated, may hold values from 0.25 to 1.75
- prompt_lengths: int32 [4], replicated, may hold values from 1 to 8192, 16384 in all
- destination: int32 [16384, 1], P(('side', 'seq')), may hold values from 0 to 127; in each aligned block of 128 rows (0 to 127, 128 to 255, ...) at most 2 rows name the same one
- request_order: int32 [128], replicated, may hold values from 0 to 127, each once
- cache: bfloat16 [128, 16384, 576], P('owner', ('side', 'seq')), may hold values from -8 to 8
- cache_lengths: int32 [128], P('owner'), may hold values from 2048 to 16384, as said below
- queries: bfloat16 [4, 128, 128, 576], P(None, 'owner'), may hold values from -32 to 32
- new_rows: bfloat16 [4, 128, 576], P(None, 'owner'), may hold values from -4 to 4
Outputs:
- attention: bfloat16 [4, 128, 128, 512], P(None, 'owner', ('side', 'seq'))
The draws below stay inside these ranges and needn't reach their ends.
Inputs may be any that keep to these rules, and one draw needn't show every extreme that they name: `destination`: within each aligned block of 128 rows no request is named by more than 2 rows, a bound that some block reaches. `request_order`: each request once. `cache_lengths`: some slot has exactly 16384 live positions. `prompt_lengths`: the prompts lie in order in the block and their lengths sum to 16384.
All inputs are finite; a program needn't handle non-finite values.
Results may differ from the reference program's by a relative error of at most 0.012.
Values may be sent and summed in bfloat16 or wider, within the bound.
A program may use at most 192 MiB of HBM per device.

```python
import math
import jax
import jax.numpy as jnp
import numpy as np
from jax import lax

D = 7168
L = 512
R = 64
H = 128
RB = 128
STEPS = 4
CACHE = 16384
PROMPTS = 4
MOST = 2
PTOK = 16384
REQS = 128


softmax_scale = 192.0 ** (-0.5)


lead_square = 37.0 / 3.0


run_square = 1.0 + 0.04 / 3.0


run_score = 28.0


def shared_plan(key):
    key = jax.random.fold_in(key, 5)
    sign_key, size_key, run_key, place_key, shift_key, power_key = jax.random.split(key, 6)
    sign_values = jnp.where(jax.random.bernoulli(sign_key, 0.5, (REQS, L + R)), 1.0, -1.0)
    leading = sign_values * jax.random.uniform(size_key, (REQS, L + R), jnp.float32, 3.0, 4.0)
    pattern = jnp.where(jnp.arange(L + R) % 2 == 0, 1.0, -1.0)
    run_row = sign_values * pattern[None, :] * jax.random.uniform(run_key, (REQS, L + R), jnp.float32, 0.8, 1.2)
    lead_place = jax.random.randint(place_key, (REQS,), 0, CACHE // 8 - 1, jnp.int32)
    head_shift = jax.random.randint(shift_key, (REQS,), 0, 8, jnp.int32)
    strength = 2.0 ** jax.random.randint(power_key, (REQS,), 1, 4, jnp.int32).astype(jnp.float32)
    return (leading, run_row, lead_place, head_shift, strength)


def draw_cache(key, part):
    leading, run_row, lead_place, head_shift, strength = shared_plan(key)
    key = jax.random.fold_in(key, 11)
    value_key, jitter_key = jax.random.split(key)
    values = jax.random.truncated_normal(value_key, -4.0, 4.0, (REQS, CACHE, L + R), jnp.float32)
    positions = jnp.arange(CACHE)
    in_run = (positions >= CACHE // 4) & (positions < CACHE // 2)
    values = jnp.where(in_run[None, :, None], run_row[:, None, :] + 0.2 * values, values)
    jitter = jax.random.normal(jitter_key, (REQS, L + R), jnp.float32)
    length_sq = jnp.sum(leading * leading, axis=1, keepdims=True)
    orthogonal = jitter - jnp.sum(jitter * leading, axis=1, keepdims=True) / length_sq * leading
    closeness = 1.0 - 2.0 / (strength[:, None] * length_sq * softmax_scale)
    partner = closeness * leading + 0.5 * orthogonal
    is_lead = positions[None, :] == lead_place[:, None]
    is_partner = positions[None, :] == lead_place[:, None] + 1
    values = jnp.where(is_lead[:, :, None], leading[:, None, :], values)
    values = jnp.where(is_partner[:, :, None], partner[:, None, :], values)
    return jnp.clip(values, -8.0, 8.0).astype(jnp.bfloat16)


def draw_queries(key, part):
    leading, run_row, lead_place, head_shift, strength = shared_plan(key)
    key = jax.random.fold_in(key, 12)
    value_key, gap_key = jax.random.split(key)
    values = 2.5 * jax.random.truncated_normal(value_key, -4.0, 4.0, (STEPS, REQS, H, L + R), jnp.float32)
    head_phase = (jnp.arange(H)[None, :] + head_shift[:, None]) % 8
    aligned = head_phase == 0
    run_heads = head_phase == 4
    score_gap = jax.random.uniform(gap_key, (STEPS, REQS, H, 1), jnp.float32, 8.5, 11.5)
    run_weight = run_score / ((L + R) * run_square * softmax_scale)
    lead_weight = (run_score + score_gap) / ((L + R) * lead_square * softmax_scale)
    mixed = lead_weight * leading[None, :, None, :] + run_weight * run_row[None, :, None, :] + 0.12 * values
    aligned_rows = (strength[:, None] * leading)[None, :, None, :]
    values = jnp.where(run_heads[None, :, :, None], mixed, values)
    values = jnp.where(aligned[None, :, :, None], aligned_rows, values)
    return jnp.clip(values, -32.0, 32.0).astype(jnp.bfloat16)


def draw_prompt_hidden(key, part):
    key = jax.random.fold_in(key, 21)
    row_key, value_key, common_key = jax.random.split(key, 3)
    values = jax.random.truncated_normal(value_key, -4.0, 4.0, (PTOK, D), jnp.float32)
    scales = jnp.exp(jax.random.uniform(row_key, (PTOK, 1), jnp.float32, math.log(0.3), math.log(3.0)))
    return (values * scales).astype(jnp.bfloat16)


def draw_latent_weight(key, part):
    key = jax.random.fold_in(key, 31)
    column_key, value_key = jax.random.split(key)
    scales = jnp.exp(jax.random.uniform(column_key, (1, L + R), jnp.float32, math.log(0.3), math.log(3.0))) / math.sqrt(D)
    values = jax.random.truncated_normal(value_key, -4.0, 4.0, (D, L + R), jnp.float32)
    return (values * scales).astype(jnp.bfloat16)


def draw_cache_lengths(key, part):
    key = jax.random.fold_in(key, 41)
    length_key, place_key = jax.random.split(key)
    lengths = jax.random.randint(length_key, (REQS,), CACHE // 8, CACHE + 1, jnp.int32)
    longest = jax.random.randint(place_key, (), 0, REQS, jnp.int32)
    return jnp.where(jnp.arange(REQS) == longest, CACHE, lengths).astype(jnp.int32)


def steps_of(rng, dims, cuts, least, largest):
    def one(dim, shards_of):
        steps = jax.random.uniform(jax.random.fold_in(jax.random.fold_in(rng, 6), dim), (shards_of,), jnp.float32, least / len(cuts), largest / len(cuts))
        return jnp.repeat(jnp.exp(steps), dims[dim] // shards_of).reshape((-1,) + (1,) * (len(dims) - dim - 1))

    gain = one(*cuts[0])
    for cut in cuts[1:]:
        gain = gain * one(*cut)
    return gain


def length_profile(amount, total, reach, skew):
    weights = [(1 << 20) // math.isqrt(rank ** skew) + 1 for rank in range(2, amount + 1)]
    surplus, holding = total - reach - (amount - 1), [1] * (amount - 1)
    while surplus > 0:
        candidates = [i for i in range(amount - 1) if holding[i] < reach]
        pool, remaining = sum([weights[i] for i in candidates]), surplus
        for i in candidates:
            extra = min(reach - holding[i], max(1, remaining * weights[i] // pool), surplus)
            holding[i] = holding[i] + extra
            surplus = surplus - extra
    return np.array([reach] + holding)


def ragged_sizes(own_key, number_of, total, most, lean):
    if number_of == 2:
        one = jax.random.randint(own_key, (), max(1, total - most), min(most, total - 1) + 1)
        return jnp.stack([one, total - one])
    sizes = jnp.asarray(length_profile(number_of, total, most, lean), jnp.int32)
    twos = (number_of - 1) // 2
    source_of, sink = sizes[1:1 + 2 * twos:2], sizes[2:2 + 2 * twos:2]
    room = jnp.minimum(source_of - 1, most - sink)
    moved = jax.random.randint(jax.random.fold_in(own_key, 1), (twos,), 0, 1 << 20) % (room + 1)
    sizes = sizes.at[1:1 + 2 * twos:2].set(source_of - moved).at[2:2 + 2 * twos:2].set(sink + moved)
    return sizes[jax.random.permutation(jax.random.fold_in(own_key, 2), number_of)]


def assign_block(rng, own, number, rows, count, top, reach, skew):
    ranking = jax.random.permutation(rng, count)
    crowded, usual = portions_of(count, rows * top, reach, skew, True), portions_of(count, rows * top, reach, skew, False)
    places = jnp.arange(count)

    def named(sizes, offset_by):
        used = int((sizes > 0).sum())
        fixed = max(1, used // 4)
        moved = fixed + (places - fixed + offset_by * (used - fixed)) % max(1, count - fixed)
        return jnp.zeros((count,), jnp.int32).at[ranking[jnp.where(places < fixed, places, moved)]].set(jnp.asarray(sizes, jnp.int32))

    sizes = jnp.where(number % 4 == 0, named(crowded, number // 4), named(usual, number - number // 4 - 1))
    mixed = jax.random.permutation(jax.random.fold_in(own, 3), count)
    donor, sink = mixed[0:count // 2 * 2:2], mixed[1:count // 2 * 2:2]
    slack = jnp.minimum(sizes[donor] - 1, reach - sizes[sink]) // 2
    slack = jnp.where((donor == ranking[0]) | (sink == ranking[0]) | (sizes[sink] == 0), 0, jnp.maximum(slack, 0))
    moved = jax.random.randint(jax.random.fold_in(own, 4), (count // 2,), 0, 1 << 20) % (slack + 1)
    sizes = sizes.at[donor].add(-moved).at[sink].add(moved)
    items = jnp.searchsorted(jnp.cumsum(sizes), jnp.arange(rows * top), side="right").astype(jnp.int32)
    table = items.reshape(top, rows).T
    table = table[jax.random.permutation(jax.random.fold_in(own, 1), rows)]
    offset_by = jax.random.randint(jax.random.fold_in(own, 2), (rows, 1), 0, top)
    return jnp.take_along_axis(table, (jnp.arange(top)[None, :] + offset_by) % top, axis=1)


def portions_of(number_of, total, bound, skew, full):
    weights = [(1 << 20) // math.isqrt(grade ** skew) + 1 for grade in range(1, number_of + 1)]
    largest = bound if full else min(bound, max(-(-total // number_of), total * weights[0] // sum(weights)))
    least = 1 if total - largest >= number_of - 1 else 0
    holding, rest = [largest] + [least] * (number_of - 1), total - largest - least * (number_of - 1)
    while rest > 0:
        movable = [i for i in range(1, number_of) if holding[i] < largest] or [i for i in range(1, number_of) if holding[i] < bound]
        mass, left = sum([weights[i] for i in movable]), rest
        for i in movable:
            addition = min(bound - holding[i], max(1, left * weights[i] // mass), rest)
            holding[i] = holding[i] + addition
            rest = rest - addition
    return np.array(holding)


def scatter_about(rng, dims, spread, limit, cuts=(), held_as=jnp.bfloat16):
    result = jax.random.normal(rng, dims, jnp.float32) * spread
    if len(cuts) > 0:
        result = steps_of(rng, dims, cuts, -0.22, 0.18) * result
    return jnp.clip(result, min=-limit, max=limit).astype(held_as)


def setup_inputs(seed: int = 0) -> dict:
    arg_keys = jax.random.split(jax.random.key(seed), 11)
    prompt_hidden = draw_prompt_hidden(jax.random.fold_in(arg_keys[10], 71), 0)
    latent_weight = draw_latent_weight(jax.random.fold_in(arg_keys[10], 71), 0)
    kv_gain = jnp.clip(1.0 + 0.15 * jax.random.normal(arg_keys[2], (L,), jnp.float32), 0.25, 1.75)
    prompt_lengths = ragged_sizes(arg_keys[3], PROMPTS, PTOK, PTOK // 2, 2).astype(jnp.int32)
    destination_keys = jax.random.split(jax.random.fold_in(arg_keys[4], 1), PTOK // RB)
    destination_turns = jax.random.permutation(jax.random.fold_in(arg_keys[4], 3), PTOK // RB)
    destination = jax.vmap(lambda own, number: assign_block(jax.random.fold_in(arg_keys[4], 2), own, number, RB, REQS, 1, MOST, 2))(destination_keys, destination_turns).reshape((PTOK, 1))
    request_order = jax.random.permutation(arg_keys[5], REQS).astype(jnp.int32)
    cache = draw_cache(jax.random.fold_in(arg_keys[10], 71), 0)
    cache_lengths = draw_cache_lengths(jax.random.fold_in(arg_keys[10], 71), 0)
    queries = draw_queries(jax.random.fold_in(arg_keys[10], 71), 0)
    new_rows = scatter_about(arg_keys[9], (STEPS, REQS, L + R), 1.0, 4.0, ((1, 32),))
    return {"prompt_hidden": prompt_hidden, "latent_weight": latent_weight, "kv_gain": kv_gain, "prompt_lengths": prompt_lengths, "destination": destination, "request_order": request_order, "cache": cache, "cache_lengths": cache_lengths, "queries": queries, "new_rows": new_rows}


softmax_scale = 192.0 ** (-0.5)
rope_theta = 10000.0
norm_eps = 1e-06
masked_score = -1e+30

def rotate_pairs(rope_part, positions):
    half_width = rope_part.shape[1] // 2
    frequency = rope_theta ** (-jnp.arange(half_width, dtype=jnp.float32) / half_width)
    angles = positions.astype(jnp.float32)[:, None] * frequency[None, :]
    cosine = jnp.cos(angles)
    sine = jnp.sin(angles)
    first_half = rope_part[:, :half_width]
    second_half = rope_part[:, half_width:]
    return jnp.concatenate([first_half * cosine - second_half * sine, first_half * sine + second_half * cosine], axis=1)

def latent_rows(projected, kv_gain, positions):
    latent_width = kv_gain.shape[0]
    latent = projected[:, :latent_width]
    mean_square = lax.optimization_barrier(jnp.mean(latent * latent, axis=1, keepdims=True))
    normed = latent * lax.rsqrt(mean_square + norm_eps) * kv_gain.astype(jnp.float32)[None, :]
    return jnp.concatenate([normed, rotate_pairs(projected[:, latent_width:], positions)], axis=1).astype(jnp.bfloat16)

def token_positions(tokens, prompt_lengths):
    starts = (jnp.cumsum(prompt_lengths) - prompt_lengths).astype(jnp.int32)
    began = jnp.where(starts[None, :] <= tokens[:, None], starts[None, :], 0).astype(jnp.int32)
    return (tokens - lax.optimization_barrier(jnp.max(began, axis=1))).astype(jnp.int32)

def reference(prompt_hidden, latent_weight, kv_gain, prompt_lengths, destination, request_order, cache, cache_lengths, queries, new_rows):
    projected = jnp.dot(prompt_hidden, latent_weight, preferred_element_type=jnp.float32)
    tokens = jnp.arange(PTOK, dtype=jnp.int32)
    handed = latent_rows(projected, kv_gain, token_positions(tokens, prompt_lengths))
    targets = destination[:, 0].astype(jnp.int32)
    sorted_order = jnp.argsort(targets, stable=True).astype(jnp.int32)
    sorted_rows = handed[sorted_order]
    request_ids = jnp.arange(REQS, dtype=jnp.int32)
    counts = lax.optimization_barrier(jnp.sum((targets[None, :] == request_ids[:, None]).astype(jnp.int32), axis=1)).astype(jnp.int32)
    firsts = (jnp.cumsum(counts) - counts).astype(jnp.int32)
    room_rows = MOST * (PTOK // RB)
    latent_width = kv_gain.shape[0]
    positions_cache = jnp.arange(CACHE, dtype=jnp.int32)
    step_order = jnp.arange(STEPS, dtype=jnp.int32)
    live_new = (step_order[None, :] <= step_order[:, None])[:, None, :]

    def one_slot(slot):
        request = request_order[slot]
        picks = jnp.arange(room_rows, dtype=jnp.int32)
        live_own = (picks < counts[request])[None, None, :]
        own_keys = sorted_rows[jnp.clip(firsts[request] + picks, 0, PTOK - 1)].astype(jnp.float32)
        query_rows = queries[:, slot].astype(jnp.float32)
        cache_keys = cache[slot].astype(jnp.float32)
        fresh_keys = new_rows[:, slot].astype(jnp.float32)
        live_cache = (positions_cache < cache_lengths[slot])[None, None, :]
        scores_cache = jnp.einsum('shk,ck->shc', query_rows, cache_keys) * softmax_scale
        scores_own = jnp.einsum('shk,ck->shc', query_rows, own_keys) * softmax_scale
        scores_new = jnp.einsum('shk,uk->shu', query_rows, fresh_keys) * softmax_scale
        top_score = jnp.maximum(lax.optimization_barrier(jnp.max(jnp.where(live_cache, scores_cache, masked_score), axis=2)), lax.optimization_barrier(jnp.max(jnp.where(live_own, scores_own, masked_score), axis=2)))
        top_score = jnp.maximum(top_score, lax.optimization_barrier(jnp.max(jnp.where(live_new, scores_new, masked_score), axis=2)))
        weights_cache = jnp.where(live_cache, jnp.exp(scores_cache - top_score[:, :, None]), 0.0)
        weights_own = jnp.where(live_own, jnp.exp(scores_own - top_score[:, :, None]), 0.0)
        weights_new = jnp.where(live_new, jnp.exp(scores_new - top_score[:, :, None]), 0.0)
        denominator = lax.optimization_barrier(jnp.sum(weights_cache, axis=2)) + lax.optimization_barrier(jnp.sum(weights_own, axis=2)) + lax.optimization_barrier(jnp.sum(weights_new, axis=2))
        accumulated = jnp.einsum('shc,cl->shl', weights_cache.astype(jnp.bfloat16).astype(jnp.float32), cache_keys[:, :latent_width])
        accumulated = accumulated + jnp.einsum('shc,cl->shl', weights_own.astype(jnp.bfloat16).astype(jnp.float32), own_keys[:, :latent_width])
        accumulated = accumulated + jnp.einsum('shu,ul->shl', weights_new.astype(jnp.bfloat16).astype(jnp.float32), fresh_keys[:, :latent_width])
        return (accumulated / denominator[:, :, None]).astype(jnp.bfloat16)
    attended = lax.map(one_slot, jnp.arange(REQS, dtype=jnp.int32))
    return jnp.transpose(attended, (1, 0, 2, 3))
```

```python
import functools

import jax
import jax.numpy as jnp
from jax import lax
from jax.experimental import pallas as pl
from jax.experimental.pallas import tpu as pltpu
from jax.sharding import PartitionSpec as P

rope_theta = 10000.0
norm_eps = 1e-06
masked_score = -1e30
score_scale = 192.0 ** (-0.5) * 1.4426950408889634

LATENT = 512
WIDTH = 576
EXT = 592
PAD = 640
HEADS = 128
KEYS = 4096
CHUNKS = 4
CHUNK = KEYS // CHUNKS
REQ = 4
ROWS = 512
PIECE = WIDTH // 4
RING_MASKS = (2, 8, 6, 24)
F32 = jnp.float32
BF16 = jnp.bfloat16


def piece_slot(piece, flips):
    slot = 0
    for i in range(4):
        slot = slot * 2 + ((flips >> ((piece + i) % 4)) & 1)
    return slot


def flips_mask(flips):
    mask = 0
    for i in range(4):
        if (flips >> i) & 1:
            mask ^= RING_MASKS[i]
    return mask


def kernel(
    lens_ref,
    plens_ref,
    hid_hbm,
    w_hbm,
    gain_ref,
    dest_ref,
    order_ref,
    cache_hbm,
    query_hbm,
    new_ref,
    out_ref,
    hid,
    w,
    wt,
    part,
    landed,
    keys,
    qraw,
    qx,
    qown,
    scores,
    tops,
    sums,
    acc,
    mstat,
    lstat,
    seq_acc,
    seq_m,
    seq_l,
    side_out,
    side_in,
    stat_out,
    stat_in,
    own_acc,
    own_m,
    own_l,
    ids,
    hand,
    outgoing,
    kown,
    in_sem,
    key_sem,
    rs_send,
    rs_recv,
    seq_send,
    seq_recv,
    side_send,
    side_recv,
    hand_send,
    hand_recv,
    a2a_send,
    a2a_recv,
    share_send,
    share_recv,
):
    side = lax.axis_index("side")
    owner = lax.axis_index("owner")
    seq = lax.axis_index("seq")
    quarter = side * 2 + seq
    y = owner % 2
    pair = owner // 2
    MESH = pl.DeviceIdType.MESH

    def flip(a, mask):
        out = a
        bit = 1
        while bit <= mask:
            if mask & bit:
                out = out + bit * (1 - 2 * ((a // bit) % 2))
            bit *= 2
        return out

    hid_copy = pltpu.make_async_copy(hid_hbm, hid, in_sem.at[0])
    w_copy = pltpu.make_async_copy(w_hbm, w, in_sem.at[1])
    q_copy = pltpu.make_async_copy(query_hbm, qraw, in_sem.at[2])

    def key_copy(r):
        return pltpu.make_async_copy(
            cache_hbm.at[r], keys.at[r % 2, pl.ds(0, WIDTH)], key_sem.at[r % 2]
        )

    hid_copy.start()
    w_copy.start()
    q_copy.start()
    key_copy(0).start()
    key_copy(1).start()

    seq_peer = (side, owner, 1 - seq)
    side_peer = (1 - side, owner, seq)
    rs_peers = [(side, flip(owner, mask), seq) for mask in RING_MASKS + (1,)]

    def a2a_target(i):
        k = i % 16
        there = (pair + k) % 16
        to_y = (y + seq) % 2
        to_side = (side + i // 16) % 2
        return (to_side, there * 2 + to_y, 1 - seq), there

    def a2a_source(i):
        k = i % 16
        there = (pair + 16 - k) % 16
        from_y = (y + 1 - seq) % 2
        from_side = (side + i // 16) % 2
        return (from_side, there * 2 + from_y, 1 - seq)

    barrier = pltpu.get_barrier_semaphore()
    for peer in rs_peers + [seq_peer, side_peer]:
        pl.semaphore_signal(barrier, inc=1, device_id=peer, device_id_type=MESH)

    def greet(i, _):
        pl.semaphore_signal(barrier, inc=1, device_id=a2a_source(i), device_id_type=MESH)
        return 0

    lax.fori_loop(0, 32, greet, 0)

    dest = dest_ref[:, pl.ds(pl.multiple_of(owner * 128, 128), 128)].astype(F32)
    dest_lane = jnp.broadcast_to(dest, (128, 128))
    dest_sub = dest_lane.T
    order_sub = jnp.broadcast_to(order_ref[...].astype(F32), (128, 128)).T
    sub = lax.broadcasted_iota(jnp.int32, (128, 128), 0)
    lane = lax.broadcasted_iota(jnp.int32, (128, 128), 1)
    slot = jnp.sum(jnp.where(order_sub == dest_lane, sub, 0), axis=0, keepdims=True)
    rank = jnp.sum(
        jnp.where((dest_sub == dest_lane) & (sub < lane), 1, 0), axis=0, keepdims=True
    )
    row_id = (slot // 4) * 16 + (slot % 4) * 4 + seq * 2 + rank
    ids[0] = jnp.broadcast_to(row_id, (8, 128))

    w_copy.wait()
    wt[...] = w[...].T
    hid_copy.wait()
    for flips in range(16):
        at = flip(owner, flips_mask(flips)) // 2
        block = jnp.dot(
            wt[...],
            hid[:, pl.ds(pl.multiple_of(at * 256, 256), 256)],
            preferred_element_type=F32,
        ).astype(BF16)
        for half in range(2):
            rel = (half + y) % 2
            for p in range(4):
                part[p, piece_slot(p, flips) * 2 + rel] = block[
                    p * PIECE : (p + 1) * PIECE, half * 128 : (half + 1) * 128
                ]

    pl.semaphore_wait(barrier, 7 + 32)

    id_copy = pltpu.make_async_remote_copy(
        ids.at[0], ids.at[1], hand_send.at[0], hand_recv.at[0], seq_peer, device_id_type=MESH
    )
    id_copy.start()

    starts = (0, 16, 24, 28, 30)

    def rs_copy(stage, p, sub_part):
        held = 32 >> stage
        if stage == 4:
            lo, n = 1, 1
            peer = rs_peers[4]
        else:
            n = held // 4
            lo = held // 2 + (n if sub_part == 0 else 0)
            peer = rs_peers[(p + stage) % 4]
        index = (stage * 2 + sub_part) * 4 + p
        return pltpu.make_async_remote_copy(
            part.at[p, pl.ds(lo, n)],
            landed.at[p, pl.ds(starts[stage] + lo - held // 2, n)],
            rs_send.at[index],
            rs_recv.at[index],
            peer,
            device_id_type=MESH,
        )

    def rs_start(stage):
        for sub_part in range(2 if stage < 4 else 1):
            for p in range(4):
                rs_copy(stage, p, sub_part).start()

    def rs_take(stage, sub_part):
        held = 32 >> stage
        n = held // 4
        lo = n if sub_part == 0 else 0
        for p in range(4):
            rs_copy(stage, p, sub_part).wait_recv()

            def add(j, _):
                part[p, lo + j] = part[p, lo + j] + landed[p, starts[stage] + lo + j]
                return 0

            lax.fori_loop(0, n, add, 0)

    def rs_first(stage):
        rs_take(stage, 0)
        rs_start(stage + 1)

    def rs_second(stage):
        rs_take(stage, 1)

    rs_start(0)

    kown[1024:1152, :] = jnp.zeros((128, PAD), BF16)
    new_all = jnp.concatenate([new_ref[u].astype(F32) for u in range(4)], axis=0)
    kown[1024:1040, 0:WIDTH] = new_all.astype(BF16)
    marks = jnp.where(
        lax.broadcasted_iota(jnp.int32, (PAD - WIDTH, 128), 0) == 0, -1.0, 0.0
    ).astype(BF16)
    for c in range(2):
        hand[c, WIDTH:PAD, :] = marks

    q_copy.wait()

    def queries_in(r):
        lead = jnp.where(
            lax.broadcasted_iota(jnp.int32, (128, EXT - WIDTH), 1) == 0, masked_score, 0.0
        ).astype(BF16)
        for s in range(4):
            rows = qraw[s, r].T
            for hq in range(4):
                rel_seq = (hq + seq) % 2
                rel_side = (hq // 2 + side) % 2
                at = pl.multiple_of((rel_seq * 2 + rel_side) * 128 + s * 32, 32)
                qx[r % 2, pl.ds(at, 32), 0:WIDTH] = rows[hq * 32 : (hq + 1) * 32]
        for s in range(4):
            qx[r % 2, s * 128 : (s + 1) * 128, WIDTH:EXT] = lead
        qown[r * 128 : (r + 1) * 128, :] = qx[r % 2, 0:128, :]

    def dead_row(r):
        place = lax.broadcasted_iota(jnp.int32, (EXT - WIDTH, KEYS), 1) + quarter * KEYS
        first = lax.broadcasted_iota(jnp.int32, (EXT - WIDTH, KEYS), 0) == 0
        keys[r % 2, WIDTH:EXT, :] = jnp.where(
            (place >= lens_ref[r]) & first, 1.0, 0.0
        ).astype(BF16)

    def seq_copies(r):
        return [
            pltpu.make_async_remote_copy(
                src.at[r, pl.ds(256, 256)],
                dst.at[r],
                seq_send.at[r * 3 + i],
                seq_recv.at[r * 3 + i],
                seq_peer,
                device_id_type=MESH,
            )
            for i, (src, dst) in enumerate(((acc, seq_acc), (mstat, seq_m), (lstat, seq_l)))
        ]

    def side_copies(r):
        return [
            pltpu.make_async_remote_copy(
                src.at[r],
                dst.at[r],
                side_send.at[r * 2 + i],
                side_recv.at[r * 2 + i],
                side_peer,
                device_id_type=MESH,
            )
            for i, (src, dst) in enumerate(((side_out, side_in), (stat_out, stat_in)))
        ]

    def seq_start(r):
        total = jnp.sum(sums[...], axis=1, keepdims=True)
        lstat[r] = jnp.broadcast_to(total, (ROWS, 128))
        for copy in seq_copies(r):
            copy.start()

    def wide(x):
        return jnp.concatenate([x] * 4, axis=1)

    def seq_join(r):
        for copy in seq_copies(r):
            copy.wait_recv()
        for half in (1, 0):
            rows = pl.ds(half * 128, 128)
            m_a, m_b = mstat[r, rows], seq_m[r, rows]
            top = jnp.maximum(m_a, m_b)
            e_a, e_b = jnp.exp2(m_a - top), jnp.exp2(m_b - top)
            total = lstat[r, rows] * e_a + seq_l[r, rows] * e_b
            joined = acc[r, rows] * wide(e_a) + seq_acc[r, rows] * wide(e_b)
            if half == 1:
                side_out[r] = joined.astype(BF16)
                eight = lax.broadcasted_iota(jnp.int32, (8, 128), 0)
                stat_out[r] = jnp.where(eight < 4, top.T[0:8], total.T[0:8])
                for copy in side_copies(r):
                    copy.start()
            else:
                own_acc[r] = joined
                own_m[r] = top
                own_l[r] = total

    def side_join(r):
        for copy in side_copies(r):
            copy.wait_recv()
        m_a = own_m[r]
        m_b = jnp.broadcast_to(stat_in[r, 0:1], (128, 128)).T
        l_b = jnp.broadcast_to(stat_in[r, 4:5], (128, 128)).T
        top = jnp.maximum(m_a, m_b)
        e_a, e_b = jnp.exp2(m_a - top), jnp.exp2(m_b - top)
        own_l[r] = own_l[r] * e_a + l_b * e_b
        own_m[r] = top
        own_acc[r] = own_acc[r] * wide(e_a) + side_in[r].astype(F32) * wide(e_b)

    def handed():
        rows = []
        for p in range(4):
            rs_copy(4, p, 0).wait_recv()
            rows.append(part[p, 0].astype(F32) + landed[p, starts[4]].astype(F32))
        row = jnp.concatenate(rows, axis=0)
        latent = row[0:LATENT]
        mean = jnp.sum(latent * latent, axis=0, keepdims=True) * (1.0 / LATENT)
        gain = jnp.broadcast_to(gain_ref[...], (128, LATENT)).T
        hand[0, 0:LATENT, :] = (latent * lax.rsqrt(mean + norm_eps) * gain).astype(BF16)
        token = (
            quarter * 4096 + owner * 128 + lax.broadcasted_iota(jnp.int32, (32, 128), 1)
        )
        began = jnp.zeros((32, 128), jnp.int32)
        start = jnp.int32(0)
        for p in range(4):
            began = jnp.maximum(began, jnp.where(start <= token, start, 0))
            start = start + plens_ref[p]
        which = lax.broadcasted_iota(jnp.int32, (32, 128), 0)
        frequency = jnp.ones((32, 128), F32)
        for i in range(1, 32):
            frequency = jnp.where(which == i, rope_theta ** (-i / 32), frequency)
        angle = (token - began).astype(F32) * frequency
        cosine, sine = jnp.cos(angle), jnp.sin(angle)
        b, c = row[LATENT : LATENT + 32], row[LATENT + 32 : WIDTH]
        hand[0, LATENT : LATENT + 32, :] = (b * cosine - c * sine).astype(BF16)
        hand[0, LATENT + 32 : WIDTH, :] = (b * sine + c * cosine).astype(BF16)

    hand_copy = pltpu.make_async_remote_copy(
        hand.at[0, pl.ds(0, WIDTH)],
        hand.at[1, pl.ds(0, WIDTH)],
        hand_send.at[1],
        hand_recv.at[1],
        seq_peer,
        device_id_type=MESH,
    )

    def pack_rows():
        packed = jnp.where(lax.broadcasted_iota(jnp.int32, (256, PAD), 1) == WIDTH, 1.0, 0.0)
        to_y = (y + seq) % 2
        for c in range(2):
            group = ids[c, 0:1] // 16
            place = jnp.where(group % 2 == to_y, (group // 2) * 16 + ids[c, 0:1] % 16, -1)
            hot = jnp.where(
                lax.broadcasted_iota(jnp.int32, (256, 128), 0) == place, 1.0, 0.0
            ).astype(BF16)
            packed = packed + lax.dot_general(
                hot, hand[c], (((1,), (1,)), ((), ())), preferred_element_type=F32
            )
        outgoing[...] = packed.astype(BF16)

    def a2a_copy(i):
        device, there = a2a_target(i)
        return pltpu.make_async_remote_copy(
            outgoing.at[pl.ds(pl.multiple_of(there * 16, 16), 16)],
            kown.at[pl.ds(pl.multiple_of(i * 16, 16), 16)],
            a2a_send.at[i],
            a2a_recv.at[i],
            device,
            device_id_type=MESH,
        )

    def share_copy(i):
        return pltpu.make_async_remote_copy(
            kown.at[pl.ds(i * 256, 256)],
            kown.at[pl.ds(512 + i * 256, 256)],
            share_send.at[i],
            share_recv.at[i],
            seq_peer,
            device_id_type=MESH,
        )

    def loop(lo, hi, f):
        def step(i, _):
            f(i)
            return 0

        lax.fori_loop(lo, hi, step, 0)

    hooks = {
        (1, 2): [lambda: rs_first(0)],
        (2, 1): [lambda: rs_second(0)],
        (2, 2): [lambda: seq_join(0)],
        (2, 3): [lambda: rs_first(1)],
        (3, 0): [lambda: rs_second(1)],
        (3, 1): [lambda: rs_first(2)],
        (3, 2): [lambda: rs_second(2), lambda: rs_first(3), lambda: seq_join(1)],
        (3, 3): [lambda: rs_second(3)],
        (4, 2): [lambda: seq_join(2)],
    }

    for r in range(REQ + 1):
        if r < REQ:
            queries_in(r)
            dead_row(r)
            tops[r % 2] = jnp.full((ROWS, 128), -3e38, F32)
            key_copy(r).wait()
        if r > 0:
            b = r - 1
            top = jnp.max(tops[b % 2], axis=1, keepdims=True) * score_scale
            mstat[b] = jnp.broadcast_to(top, (ROWS, 128))
            sums[...] = jnp.zeros((ROWS, 128), F32)
            acc[b] = jnp.zeros((ROWS, LATENT), F32)

        def chunk(c, _):
            for (hook_r, hook_c), acts in hooks.items():
                if hook_r == r:

                    @pl.when(c == hook_c)
                    def _():
                        for act in acts:
                            act()

            at = pl.ds(pl.multiple_of(c * CHUNK, CHUNK), CHUNK)
            if r < REQ:
                fresh = jnp.dot(qx[r % 2], keys[r % 2, :, at], preferred_element_type=F32)
                scores[r % 2, :, at] = fresh
                top = tops[r % 2]
                for j in range(CHUNK // 128):
                    top = jnp.maximum(top, fresh[:, j * 128 : (j + 1) * 128])
                tops[r % 2] = top
            if r > 0:
                b = r - 1
                m = mstat[b]
                ready = scores[b % 2, :, at]
                weights = [
                    jnp.exp2(ready[:, j * 128 : (j + 1) * 128] * score_scale - m)
                    for j in range(CHUNK // 128)
                ]
                sums[...] += functools.reduce(jnp.add, weights)
                acc[b] += lax.dot_general(
                    jnp.concatenate(weights, axis=1).astype(BF16),
                    keys[b % 2, 0:LATENT, at],
                    (((1,), (1,)), ((), ())),
                    preferred_element_type=F32,
                )
            return 0

        lax.fori_loop(0, CHUNKS, chunk, 0)
        if r > 0:
            seq_start(r - 1)
            if r + 1 < REQ:
                key_copy(r + 1).start()

    handed()
    hand_copy.start()
    seq_join(3)
    side_join(0)
    id_copy.wait_recv()
    hand_copy.wait_recv()
    pack_rows()
    loop(0, 32, lambda i: a2a_copy(i).start())
    side_join(1)
    side_join(2)
    side_join(3)
    loop(0, 16, lambda i: a2a_copy(i).wait_recv())
    share_copy(0).start()
    loop(16, 32, lambda i: a2a_copy(i).wait_recv())
    share_copy(1).start()
    share_copy(0).wait_recv()
    share_copy(1).wait_recv()

    own_scores = lax.dot_general(
        qown[...], kown[:, 0:EXT], (((1,), (1,)), ((), ())), preferred_element_type=F32
    )
    column = lax.broadcasted_iota(jnp.int32, (1, 1024), 1)
    new_column = lax.broadcasted_iota(jnp.int32, (128, 128), 1)
    new_step = lax.broadcasted_iota(jnp.int32, (128, 128), 0) // 32
    for r in range(REQ):
        rows = own_scores[r * 128 : (r + 1) * 128]
        old = jnp.where((column // 4) % 4 == r, rows[:, 0:1024], masked_score)
        live = (new_column < 16) & (new_column % 4 == r) & (new_column // 4 <= new_step)
        late = jnp.where(live, rows[:, 1024:1152], masked_score)
        everything = jnp.concatenate([old, late], axis=1) * score_scale
        m_b = jnp.max(everything, axis=1, keepdims=True)
        weights = jnp.exp2(everything - m_b)
        l_b = jnp.sum(weights, axis=1, keepdims=True)
        acc_b = jnp.dot(weights.astype(BF16), kown[:, 0:LATENT], preferred_element_type=F32)
        m_a = own_m[r][:, 0:1]
        l_a = own_l[r][:, 0:1]
        top = jnp.maximum(m_a, m_b)
        e_a, e_b = jnp.exp2(m_a - top), jnp.exp2(m_b - top)
        total = l_a * e_a + l_b * e_b
        result = (own_acc[r] * e_a + acc_b * e_b) / total
        for s in range(4):
            out_ref[s, r] = result[s * 32 : (s + 1) * 32].astype(BF16)

    for stage in range(5):
        for sub_part in range(2 if stage < 4 else 1):
            for p in range(4):
                rs_copy(stage, p, sub_part).wait_send()
    for r in range(REQ):
        for copy in seq_copies(r) + side_copies(r):
            copy.wait_send()
    id_copy.wait_send()
    hand_copy.wait_send()
    loop(0, 32, lambda i: a2a_copy(i).wait_send())
    share_copy(0).wait_send()
    share_copy(1).wait_send()


def on_device(
    prompt_hidden,
    latent_weight,
    kv_gain,
    prompt_lengths,
    destination,
    request_order,
    cache,
    cache_lengths,
    queries,
    new_rows,
):
    smem = pl.BlockSpec(memory_space=pltpu.SMEM)
    vmem = pl.BlockSpec(memory_space=pltpu.VMEM)
    hbm = pl.BlockSpec(memory_space=pl.ANY)
    dma = pltpu.SemaphoreType.DMA
    return pl.pallas_call(
        kernel,
        out_shape=jax.ShapeDtypeStruct((4, 4, 32, LATENT), BF16),
        in_specs=[smem, smem, hbm, hbm, vmem, vmem, vmem, hbm, hbm, vmem],
        out_specs=vmem,
        scratch_shapes=[
            pltpu.VMEM((224, 4096), BF16),
            pltpu.VMEM((224, WIDTH), BF16),
            pltpu.VMEM((WIDTH, 224), BF16),
            pltpu.VMEM((4, 32, PIECE, 128), BF16),
            pltpu.VMEM((4, 31, PIECE, 128), BF16),
            pltpu.VMEM((2, EXT, KEYS), BF16),
            pltpu.VMEM((4, 4, WIDTH, HEADS), BF16),
            pltpu.VMEM((2, ROWS, EXT), BF16),
            pltpu.VMEM((ROWS, EXT), BF16),
            pltpu.VMEM((2, ROWS, KEYS), F32),
            pltpu.VMEM((2, ROWS, 128), F32),
            pltpu.VMEM((ROWS, 128), F32),
            pltpu.VMEM((REQ, ROWS, LATENT), F32),
            pltpu.VMEM((REQ, ROWS, 128), F32),
            pltpu.VMEM((REQ, ROWS, 128), F32),
            pltpu.VMEM((REQ, 256, LATENT), F32),
            pltpu.VMEM((REQ, 256, 128), F32),
            pltpu.VMEM((REQ, 256, 128), F32),
            pltpu.VMEM((REQ, 128, LATENT), BF16),
            pltpu.VMEM((REQ, 128, LATENT), BF16),
            pltpu.VMEM((REQ, 8, 128), F32),
            pltpu.VMEM((REQ, 8, 128), F32),
            pltpu.VMEM((REQ, 128, LATENT), F32),
            pltpu.VMEM((REQ, 128, 128), F32),
            pltpu.VMEM((REQ, 128, 128), F32),
            pltpu.VMEM((2, 8, 128), jnp.int32),
            pltpu.VMEM((2, PAD, 128), BF16),
            pltpu.VMEM((256, PAD), BF16),
            pltpu.VMEM((1152, PAD), BF16),
            dma((3,)),
            dma((2,)),
            dma((36,)),
            dma((36,)),
            dma((12,)),
            dma((12,)),
            dma((8,)),
            dma((8,)),
            dma((2,)),
            dma((2,)),
            dma((32,)),
            dma((32,)),
            dma((2,)),
            dma((2,)),
        ],
        compiler_params=pltpu.CompilerParams(
            collective_id=0, has_side_effects=True, vmem_limit_bytes=62 << 20
        ),
        cost_estimate=pl.CostEstimate(
            flops=20_000_000_000, bytes_accessed=24_000_000, transcendentals=8_400_000
        ),
    )(
        cache_lengths,
        prompt_lengths,
        prompt_hidden.T,
        latent_weight,
        kv_gain.reshape(1, LATENT),
        destination.T,
        request_order.reshape(1, 128),
        jnp.transpose(cache, (0, 2, 1)),
        jnp.transpose(queries, (0, 1, 3, 2)),
        new_rows,
    )


def solution(mesh):
    return jax.shard_map(
        on_device,
        mesh=mesh,
        in_specs=(
            P(("side", "seq"), "owner"),
            P("owner", None),
            P(),
            P(),
            P(("side", "seq"), None),
            P(),
            P("owner", ("side", "seq"), None),
            P("owner"),
            P(None, "owner", None, None),
            P(None, "owner", None),
        ),
        out_specs=P(None, "owner", ("side", "seq"), None),
        check_vma=False,
    )
```

```python
import functools

import jax
import jax.numpy as jnp
from jax import lax
from jax.experimental import pallas as pl
from jax.experimental.pallas import tpu as pltpu
from jax.sharding import PartitionSpec as P

rope_theta = 10000.0
norm_eps = 1e-06
masked_score = -1e30
score_scale = 192.0 ** (-0.5) * 1.4426950408889634

LATENT = 512
WIDTH = 576
EXT = 592
PAD = 640
HEADS = 128
KEYS = 4096
CHUNKS = (4, 4, 4, 8, 8)
CUTS = (4, 6)
REQ = 4
ROWS = 512
PIECE = WIDTH // 4
NEW = 512
OTHER = NEW + 128
RING_MASKS = (2, 8, 6, 24)
F32 = jnp.float32
BF16 = jnp.bfloat16


def piece_slot(piece, flips):
    slot = 0
    for i in range(4):
        slot = slot * 2 + ((flips >> ((piece + i) % 4)) & 1)
    return slot


def flips_mask(flips):
    mask = 0
    for i in range(4):
        if (flips >> i) & 1:
            mask ^= RING_MASKS[i]
    return mask


def kernel(
    lens_ref,
    plens_ref,
    hid_hbm,
    w_hbm,
    gain_ref,
    dest_ref,
    order_ref,
    cache_hbm,
    query_hbm,
    new_ref,
    out_ref,
    hid,
    w,
    wt,
    part,
    landed,
    keys,
    qraw,
    qx,
    qown,
    scores,
    tops,
    sums,
    acc,
    mstat,
    lstat,
    seq_out,
    seq_in,
    seq_stat,
    seq_stat_in,
    side_out,
    side_in,
    stat_out,
    stat_in,
    own_acc,
    own_m,
    own_l,
    ids,
    hand,
    outgoing,
    kown,
    gain_wide,
    turn,
    hot,
    in_sem,
    key_sem,
    rs_send,
    rs_recv,
    seq_send,
    seq_recv,
    side_send,
    side_recv,
    hand_send,
    hand_recv,
    a2a_send,
    a2a_recv,
    share_send,
    share_recv,
    ready,
):
    side = lax.axis_index("side")
    owner = lax.axis_index("owner")
    seq = lax.axis_index("seq")
    quarter = side * 2 + seq
    y = owner % 2
    pair = owner // 2
    MESH = pl.DeviceIdType.MESH

    def flip(a, mask):
        out = a
        bit = 1
        while bit <= mask:
            if mask & bit:
                out = out + bit * (1 - 2 * ((a // bit) % 2))
            bit *= 2
        return out

    seq_peer = (side, owner, 1 - seq)
    side_peer = (1 - side, owner, seq)
    rs_peers = [(side, flip(owner, mask), seq) for mask in RING_MASKS + (1,)]

    def a2a_target(i):
        k = i % 16
        there = (pair + k) % 16
        to_y = (y + seq) % 2
        to_side = (side + i // 16) % 2
        return (to_side, there * 2 + to_y, 1 - seq), there

    barrier = pltpu.get_barrier_semaphore()
    for peer in rs_peers + [seq_peer, side_peer]:
        pl.semaphore_signal(barrier, inc=1, device_id=peer, device_id_type=MESH)


    hid_copy = pltpu.make_async_copy(hid_hbm, hid, in_sem.at[0])
    w_copy = pltpu.make_async_copy(w_hbm, w, in_sem.at[1])
    q_copy = pltpu.make_async_copy(query_hbm, qraw, in_sem.at[2])

    def key_copy(r):
        return pltpu.make_async_copy(
            cache_hbm.at[r], keys.at[r % 2, pl.ds(0, WIDTH)], key_sem.at[r % 2]
        )

    w_copy.start()
    hid_copy.start()

    dest = dest_ref[:, pl.ds(pl.multiple_of(owner * 128, 128), 128)].astype(F32)
    dest_lane = jnp.broadcast_to(dest, (128, 128))
    dest_sub = dest_lane.T
    order_sub = jnp.broadcast_to(order_ref[...].astype(F32), (128, 128)).T
    sub = lax.broadcasted_iota(jnp.int32, (128, 128), 0)
    lane = lax.broadcasted_iota(jnp.int32, (128, 128), 1)
    slot = jnp.sum(jnp.where(order_sub == dest_lane, sub, 0), axis=0, keepdims=True)
    rank = jnp.sum(
        jnp.where((dest_sub == dest_lane) & (sub < lane), 1, 0), axis=0, keepdims=True
    )
    row_id = (slot // 4) * 16 + (slot % 4) * 4 + seq * 2 + rank
    ids[0] = jnp.broadcast_to(row_id, (8, 128))

    w_copy.wait()
    wt[...] = w[...].T
    hid_copy.wait()
    q_copy.start()
    key_copy(0).start()
    key_copy(1).start()

    def project(flips):
        at = flip(owner, flips_mask(flips)) // 2
        block = jnp.dot(
            wt[...],
            hid[:, pl.ds(pl.multiple_of(at * 256, 256), 256)],
            preferred_element_type=F32,
        ).astype(BF16)
        for half in range(2):
            rel = (half + y) % 2
            for p in range(4):
                part[p, piece_slot(p, flips) * 2 + rel] = block[
                    p * PIECE : (p + 1) * PIECE, half * 128 : (half + 1) * 128
                ]

    starts = (0, 16, 24, 28, 30)

    def rs_copy(stage, p, sub_part):
        held = 32 >> stage
        if stage == 4:
            lo, n = 1, 1
            peer = rs_peers[4]
        else:
            n = held // 4
            lo = held // 2 + (n if sub_part == 0 else 0)
            peer = rs_peers[(p + stage) % 4]
        index = (stage * 2 + sub_part) * 4 + p
        return pltpu.make_async_remote_copy(
            part.at[p, pl.ds(lo, n)],
            landed.at[p, pl.ds(starts[stage] + lo - held // 2, n)],
            rs_send.at[index],
            rs_recv.at[index],
            peer,
            device_id_type=MESH,
        )

    def rs_part(stage, sub_part):
        for p in range(4):
            rs_copy(stage, p, sub_part).start()

    def rs_start(stage):
        rs_part(stage, 0)
        if stage < 4:
            rs_part(stage, 1)

    def rs_take(stage, sub_part):
        held = 32 >> stage
        n = held // 4
        lo = n if sub_part == 0 else 0
        for p in range(4):
            rs_copy(stage, p, sub_part).wait_recv()

            def add(j, _):
                part[p, lo + j] = part[p, lo + j] + landed[p, starts[stage] + lo + j]
                return 0

            lax.fori_loop(0, n, add, 0)

    def rs_first(stage):
        rs_take(stage, 0)
        rs_start(stage + 1)

    def rs_second(stage):
        rs_take(stage, 1)

    for flips in (15, 7, 11, 13, 14, 3, 6, 12, 9):
        project(flips)
    pl.semaphore_wait(barrier, 7)
    rs_part(0, 0)
    for flips in (5, 10, 1, 2, 4, 8, 0):
        project(flips)
    rs_part(0, 1)
    id_copy = pltpu.make_async_remote_copy(
        ids.at[0], ids.at[1], hand_send.at[0], hand_recv.at[0], seq_peer, device_id_type=MESH
    )
    id_copy.start()

    kown[NEW : NEW + 128, :] = jnp.zeros((128, PAD), BF16)
    new_all = jnp.concatenate([new_ref[u].astype(F32) for u in range(4)], axis=0)
    kown[NEW : NEW + 16, 0:WIDTH] = new_all.astype(BF16)
    marks = jnp.where(
        lax.broadcasted_iota(jnp.int32, (PAD - WIDTH, 128), 0) == 0, -1.0, 0.0
    ).astype(BF16)
    for c in range(2):
        hand[c, WIDTH:PAD, :] = marks

    q_copy.wait()

    def queries_in(r):
        lead = jnp.where(
            lax.broadcasted_iota(jnp.int32, (128, EXT - WIDTH), 1) == 0, masked_score, 0.0
        ).astype(BF16)
        for s in range(4):
            rows = qraw[s, r].T
            for hq in range(4):
                rel_seq = (hq + seq) % 2
                rel_side = (hq // 2 + side) % 2
                at = pl.multiple_of((rel_seq * 2 + rel_side) * 128 + s * 32, 32)
                qx[r % 2, pl.ds(at, 32), 0:WIDTH] = rows[hq * 32 : (hq + 1) * 32]
        for s in range(4):
            qx[r % 2, s * 128 : (s + 1) * 128, WIDTH:EXT] = lead
        qown[r * 128 : (r + 1) * 128, :] = qx[r % 2, 0:128, :]

    def dead_row(r):
        place = lax.broadcasted_iota(jnp.int32, (EXT - WIDTH, KEYS), 1) + quarter * KEYS
        first = lax.broadcasted_iota(jnp.int32, (EXT - WIDTH, KEYS), 0) == 0
        keys[r % 2, WIDTH:EXT, :] = jnp.where(
            (place >= lens_ref[r]) & first, 1.0, 0.0
        ).astype(BF16)

    def seq_copies(r):
        return [
            pltpu.make_async_remote_copy(
                src.at[r],
                dst.at[r],
                seq_send.at[r * 2 + i],
                seq_recv.at[r * 2 + i],
                seq_peer,
                device_id_type=MESH,
            )
            for i, (src, dst) in enumerate(((seq_out, seq_in), (seq_stat, seq_stat_in)))
        ]

    def compact(m, total):
        eight = lax.broadcasted_iota(jnp.int32, (8, 128), 0)
        return jnp.where(eight < 4, m.T[0:8], total.T[0:8])

    def spread(tile):
        return (
            jnp.broadcast_to(tile[0:1], (128, 128)).T,
            jnp.broadcast_to(tile[4:5], (128, 128)).T,
        )

    def side_copies(r):
        return [
            pltpu.make_async_remote_copy(
                src.at[r],
                dst.at[r],
                side_send.at[r * 2 + i],
                side_recv.at[r * 2 + i],
                side_peer,
                device_id_type=MESH,
            )
            for i, (src, dst) in enumerate(((side_out, side_in), (stat_out, stat_in)))
        ]

    def seq_start(r):
        total = jnp.sum(sums[...], axis=1, keepdims=True)
        lstat[r] = jnp.broadcast_to(total, (ROWS, 128))
        for half in range(2):
            rows = pl.ds(256 + half * 128, 128)
            seq_out[r, half] = acc[r, rows].astype(BF16)
            seq_stat[r, half] = compact(mstat[r, rows], lstat[r, rows])
        for copy in seq_copies(r):
            copy.start()

    def wide(x):
        return jnp.concatenate([x] * 4, axis=1)

    def seq_join(r):
        for copy in seq_copies(r):
            copy.wait_recv()
        for half in (1, 0):
            rows = pl.ds(half * 128, 128)
            m_a, l_a = mstat[r, rows], lstat[r, rows]
            m_b, l_b = spread(seq_stat_in[r, half])
            top = jnp.maximum(m_a, m_b)
            e_a, e_b = jnp.exp2(m_a - top), jnp.exp2(m_b - top)
            total = l_a * e_a + l_b * e_b
            joined = acc[r, rows] * wide(e_a) + seq_in[r, half].astype(F32) * wide(e_b)
            if half == 1:
                side_out[r] = joined.astype(BF16)
                stat_out[r] = compact(top, total)
                for copy in side_copies(r):
                    copy.start()
            else:
                own_acc[r] = joined
                own_m[r] = top
                own_l[r] = total

    def side_join(r):
        for copy in side_copies(r):
            copy.wait_recv()
        m_a = own_m[r]
        m_b, l_b = spread(stat_in[r])
        top = jnp.maximum(m_a, m_b)
        e_a, e_b = jnp.exp2(m_a - top), jnp.exp2(m_b - top)
        own_l[r] = own_l[r] * e_a + l_b * e_b
        own_m[r] = top
        own_acc[r] = own_acc[r] * wide(e_a) + side_in[r].astype(F32) * wide(e_b)

    def before_handing():
        gain_wide[...] = jnp.broadcast_to(gain_ref[...], (128, LATENT)).T
        token = (
            quarter * 4096 + owner * 128 + lax.broadcasted_iota(jnp.int32, (32, 128), 1)
        )
        began = jnp.zeros((32, 128), jnp.int32)
        start = jnp.int32(0)
        for p in range(4):
            began = jnp.maximum(began, jnp.where(start <= token, start, 0))
            start = start + plens_ref[p]
        which = lax.broadcasted_iota(jnp.int32, (32, 128), 0)
        frequency = jnp.ones((32, 128), F32)
        for i in range(1, 32):
            frequency = jnp.where(which == i, rope_theta ** (-i / 32), frequency)
        angle = (token - began).astype(F32) * frequency
        turn[0] = jnp.cos(angle)
        turn[1] = jnp.sin(angle)

    def places():
        id_copy.wait_recv()
        to_y = (y + seq) % 2
        for c in range(2):
            group = ids[c, 0:1] // 16
            place = jnp.where(group % 2 == to_y, (group // 2) * 16 + ids[c, 0:1] % 16, -1)
            hot[c] = jnp.where(
                lax.broadcasted_iota(jnp.int32, (256, 128), 0) == place, 1.0, 0.0
            ).astype(BF16)

    def handed():
        rows = []
        for p in range(4):
            rs_copy(4, p, 0).wait_recv()
            rows.append(part[p, 0].astype(F32) + landed[p, starts[4]].astype(F32))
        row = jnp.concatenate(rows, axis=0)
        latent = row[0:LATENT]
        mean = jnp.sum(latent * latent, axis=0, keepdims=True) * (1.0 / LATENT)
        hand[0, 0:LATENT, :] = (latent * lax.rsqrt(mean + norm_eps) * gain_wide[...]).astype(BF16)
        cosine, sine = turn[0], turn[1]
        b, c = row[LATENT : LATENT + 32], row[LATENT + 32 : WIDTH]
        hand[0, LATENT : LATENT + 32, :] = (b * cosine - c * sine).astype(BF16)
        hand[0, LATENT + 32 : WIDTH, :] = (b * sine + c * cosine).astype(BF16)

    hand_copy = pltpu.make_async_remote_copy(
        hand.at[0, pl.ds(0, WIDTH)],
        hand.at[1, pl.ds(0, WIDTH)],
        hand_send.at[1],
        hand_recv.at[1],
        seq_peer,
        device_id_type=MESH,
    )

    def pack_rows():
        packed = jnp.where(lax.broadcasted_iota(jnp.int32, (256, PAD), 1) == WIDTH, 1.0, 0.0)
        for c in range(2):
            packed = packed + lax.dot_general(
                hot[c], hand[c], (((1,), (1,)), ((), ())), preferred_element_type=F32
            )
        outgoing[...] = packed.astype(BF16)

    def a2a_copy(i):
        device, there = a2a_target(i)
        return pltpu.make_async_remote_copy(
            outgoing.at[pl.ds(pl.multiple_of(there * 16, 16), 16)],
            kown.at[pl.ds(pl.multiple_of(i * 16 + (i // 16) * (OTHER - 256), 16), 16)],
            a2a_send.at[i],
            a2a_recv.at[i],
            device,
            device_id_type=MESH,
        )

    def share_copy(i):
        return pltpu.make_async_remote_copy(
            kown.at[pl.ds(i * OTHER, 256)],
            kown.at[pl.ds(i * OTHER + 256, 256)],
            share_send.at[i],
            share_recv.at[i],
            seq_peer,
            device_id_type=MESH,
        )

    def own_part(lo, n):
        part_scores = lax.dot_general(
            qown[...],
            kown[lo : lo + n, 0:EXT],
            (((1,), (1,)), ((), ())),
            preferred_element_type=F32,
        )
        column = lax.broadcasted_iota(jnp.int32, (1, 512), 1)
        new_column = lax.broadcasted_iota(jnp.int32, (128, 128), 1)
        new_step = lax.broadcasted_iota(jnp.int32, (128, 128), 0) // 32
        for r in range(REQ):
            rows = part_scores[r * 128 : (r + 1) * 128]
            masked = jnp.where((column // 4) % 4 == r, rows[:, 0:512], masked_score)
            if n > 512:
                live = (new_column < 16) & (new_column % 4 == r) & (new_column // 4 <= new_step)
                late = jnp.where(live, rows[:, 512:n], masked_score)
                masked = jnp.concatenate([masked, late], axis=1)
            masked = masked * score_scale
            m_a = own_m[r]
            top = jnp.maximum(m_a, jnp.max(masked, axis=1, keepdims=True))
            e_a = jnp.exp2(m_a - top)
            weights = jnp.exp2(masked - top[:, 0:1])
            own_m[r] = top
            own_l[r] = own_l[r] * e_a + jnp.sum(weights, axis=1, keepdims=True)
            own_acc[r] = own_acc[r] * wide(e_a) + jnp.dot(
                weights.astype(BF16), kown[lo : lo + n, 0:LATENT], preferred_element_type=F32
            )

    def loop(lo, hi, f):
        def step(i, _):
            f(i)
            return 0

        lax.fori_loop(lo, hi, step, 0)

    hooks = {
        (0, 2): [before_handing],
        (1, 0): [places],
        (1, 1): [lambda: rs_first(0)],
        (2, 1): [lambda: rs_second(0)],
        (2, 2): [lambda: rs_first(1), lambda: seq_join(0)],
        (3, 0): [lambda: rs_second(1)],
        (3, 1): [lambda: rs_first(2)],
        (3, 2): [lambda: seq_join(1)],
        (3, 3): [lambda: rs_second(2)],
        (3, 4): [lambda: rs_first(3)],
        (3, 6): [lambda: rs_second(3)],
        (4, 1): [lambda: side_join(0)],
        (4, 2): [lambda: seq_join(2)],
    }

    def phase(r, first, last):
        step = KEYS // CHUNKS[r]

        def chunk(c, _):
            for (hook_r, hook_c), acts in hooks.items():
                if hook_r == r:

                    @pl.when(c == hook_c)
                    def _():
                        for act in acts:
                            act()

            at = pl.ds(pl.multiple_of(c * step, step), step)
            if r < REQ:
                fresh = jnp.dot(qx[r % 2], keys[r % 2, :, at], preferred_element_type=F32)
                scores[r % 2, :, at] = fresh
                top = tops[r % 2]
                for j in range(step // 128):
                    top = jnp.maximum(top, fresh[:, j * 128 : (j + 1) * 128])
                tops[r % 2] = top
            if r > 0:
                b = r - 1
                m = mstat[b]
                ready = scores[b % 2, :, at]
                weights = [
                    jnp.exp2(ready[:, j * 128 : (j + 1) * 128] * score_scale - m)
                    for j in range(step // 128)
                ]
                sums[...] += functools.reduce(jnp.add, weights)
                acc[b] += lax.dot_general(
                    jnp.concatenate(weights, axis=1).astype(BF16),
                    keys[b % 2, 0:LATENT, at],
                    (((1,), (1,)), ((), ())),
                    preferred_element_type=F32,
                )
            return 0

        lax.fori_loop(first, last, chunk, 0)

    for r in range(REQ + 1):
        if r < REQ:
            queries_in(r)
            dead_row(r)
            tops[r % 2] = jnp.full((ROWS, 128), -3e38, F32)
            key_copy(r).wait()
        if r > 0:
            b = r - 1
            top = jnp.max(tops[b % 2], axis=1, keepdims=True) * score_scale
            mstat[b] = jnp.broadcast_to(top, (ROWS, 128))
            sums[...] = jnp.zeros((ROWS, 128), F32)
            acc[b] = jnp.zeros((ROWS, LATENT), F32)

        phase(r, 0, CHUNKS[r] if r < REQ else CUTS[0])
        if 0 < r < REQ:
            seq_start(r - 1)
            if r + 1 < REQ:
                key_copy(r + 1).start()

    handed()
    hand_copy.start()
    phase(REQ, CUTS[0], CUTS[1])
    hand_copy.wait_recv()
    pl.semaphore_signal(ready, inc=1, device_id=side_peer, device_id_type=MESH)
    pack_rows()
    loop(0, 16, lambda i: a2a_copy(i).start())
    pl.semaphore_wait(ready, 1)
    loop(16, 32, lambda i: a2a_copy(i).start())
    phase(REQ, CUTS[1], CHUNKS[REQ])
    seq_start(3)
    side_join(1)
    side_join(2)
    loop(0, 16, lambda i: a2a_copy(i).wait_recv())
    share_copy(0).start()
    seq_join(3)
    share_copy(0).wait_recv()
    own_part(0, OTHER)
    loop(16, 32, lambda i: a2a_copy(i).wait_recv())
    share_copy(1).start()
    side_join(3)
    share_copy(1).wait_recv()
    own_part(OTHER, 512)
    for r in range(REQ):
        result = own_acc[r] / wide(own_l[r])
        for s in range(4):
            out_ref[s, r] = result[s * 32 : (s + 1) * 32].astype(BF16)

    for stage in range(5):
        for sub_part in range(2 if stage < 4 else 1):
            for p in range(4):
                rs_copy(stage, p, sub_part).wait_send()
    for r in range(REQ):
        for copy in seq_copies(r) + side_copies(r):
            copy.wait_send()
    id_copy.wait_send()
    hand_copy.wait_send()
    loop(0, 32, lambda i: a2a_copy(i).wait_send())
    share_copy(0).wait_send()
    share_copy(1).wait_send()


def on_device(
    prompt_hidden,
    latent_weight,
    kv_gain,
    prompt_lengths,
    destination,
    request_order,
    cache,
    cache_lengths,
    queries,
    new_rows,
):
    smem = pl.BlockSpec(memory_space=pltpu.SMEM)
    vmem = pl.BlockSpec(memory_space=pltpu.VMEM)
    hbm = pl.BlockSpec(memory_space=pl.ANY)
    dma = pltpu.SemaphoreType.DMA
    return pl.pallas_call(
        kernel,
        out_shape=jax.ShapeDtypeStruct((4, 4, 32, LATENT), BF16),
        in_specs=[smem, smem, hbm, hbm, vmem, vmem, vmem, hbm, hbm, vmem],
        out_specs=vmem,
        scratch_shapes=[
            pltpu.VMEM((224, 4096), BF16),
            pltpu.VMEM((224, WIDTH), BF16),
            pltpu.VMEM((WIDTH, 224), BF16),
            pltpu.VMEM((4, 32, PIECE, 128), BF16),
            pltpu.VMEM((4, 31, PIECE, 128), BF16),
            pltpu.VMEM((2, EXT, KEYS), BF16),
            pltpu.VMEM((4, 4, WIDTH, HEADS), BF16),
            pltpu.VMEM((2, ROWS, EXT), BF16),
            pltpu.VMEM((ROWS, EXT), BF16),
            pltpu.VMEM((2, ROWS, KEYS), F32),
            pltpu.VMEM((2, ROWS, 128), F32),
            pltpu.VMEM((ROWS, 128), F32),
            pltpu.VMEM((REQ, ROWS, LATENT), F32),
            pltpu.VMEM((REQ, ROWS, 128), F32),
            pltpu.VMEM((REQ, ROWS, 128), F32),
            pltpu.VMEM((REQ, 2, 128, LATENT), BF16),
            pltpu.VMEM((REQ, 2, 128, LATENT), BF16),
            pltpu.VMEM((REQ, 2, 8, 128), F32),
            pltpu.VMEM((REQ, 2, 8, 128), F32),
            pltpu.VMEM((REQ, 128, LATENT), BF16),
            pltpu.VMEM((REQ, 128, LATENT), BF16),
            pltpu.VMEM((REQ, 8, 128), F32),
            pltpu.VMEM((REQ, 8, 128), F32),
            pltpu.VMEM((REQ, 128, LATENT), F32),
            pltpu.VMEM((REQ, 128, 128), F32),
            pltpu.VMEM((REQ, 128, 128), F32),
            pltpu.VMEM((2, 8, 128), jnp.int32),
            pltpu.VMEM((2, PAD, 128), BF16),
            pltpu.VMEM((256, PAD), BF16),
            pltpu.VMEM((1152, PAD), BF16),
            pltpu.VMEM((LATENT, 128), F32),
            pltpu.VMEM((2, 32, 128), F32),
            pltpu.VMEM((2, 256, 128), BF16),
            dma((3,)),
            dma((2,)),
            dma((36,)),
            dma((36,)),
            dma((8,)),
            dma((8,)),
            dma((8,)),
            dma((8,)),
            dma((2,)),
            dma((2,)),
            dma((32,)),
            dma((32,)),
            dma((2,)),
            dma((2,)),
            pltpu.SemaphoreType.REGULAR,
        ],
        compiler_params=pltpu.CompilerParams(
            collective_id=0, has_side_effects=True, vmem_limit_bytes=62 << 20
        ),
        cost_estimate=pl.CostEstimate(
            flops=20_000_000_000, bytes_accessed=24_000_000, transcendentals=8_400_000
        ),
    )(
        cache_lengths,
        prompt_lengths,
        prompt_hidden.T,
        latent_weight,
        kv_gain.reshape(1, LATENT),
        destination.T,
        request_order.reshape(1, 128),
        jnp.transpose(cache, (0, 2, 1)),
        jnp.transpose(queries, (0, 1, 3, 2)),
        new_rows,
    )


def solution(mesh):
    return jax.shard_map(
        on_device,
        mesh=mesh,
        in_specs=(
            P(("side", "seq"), "owner"),
            P("owner", None),
            P(),
            P(),
            P(("side", "seq"), None),
            P(),
            P("owner", ("side", "seq"), None),
            P("owner"),
            P(None, "owner", None, None),
            P(None, "owner", None),
        ),
        out_specs=P(None, "owner", ("side", "seq"), None),
        check_vma=False,
    )
```

```python
import functools

import jax
import jax.numpy as jnp
from jax import lax
from jax.experimental import pallas as pl
from jax.experimental.pallas import tpu as pltpu
from jax.sharding import PartitionSpec as P

rope_theta = 10000.0
norm_eps = 1e-06
masked_score = -1e30
score_scale = 192.0 ** (-0.5) * 1.4426950408889634

LATENT = 512
WIDTH = 576
EXT = 592
PAD = 640
HEADS = 128
KEYS = 4096
CHUNKS = (4, 4, 4, 4)
CUTS = (3, 3)
REQ = 4
ROWS = 512
PIECE = WIDTH // 4
NEW = 512
OTHER = NEW + 128
EARLY_Y = 3
RING_MASKS = (2, 8, 6, 24)
F32 = jnp.float32
BF16 = jnp.bfloat16


def piece_slot(piece, flips, y_flip):
    slot = 0
    for i in range(4):
        if i == 3 and piece == EARLY_Y:
            slot = slot * 2 + y_flip
        slot = slot * 2 + ((flips >> ((piece + i) % 4)) & 1)
    return slot if piece == EARLY_Y else slot * 2 + y_flip


def flips_mask(flips):
    mask = 0
    for i in range(4):
        if (flips >> i) & 1:
            mask ^= RING_MASKS[i]
    return mask


def kernel(
    lens_ref,
    plens_ref,
    hid_hbm,
    w_hbm,
    gain_ref,
    dest_ref,
    order_ref,
    cache_hbm,
    query_hbm,
    new_ref,
    out_ref,
    hid,
    w,
    wt,
    part,
    landed,
    keys,
    qraw,
    qx,
    qown,
    scores,
    tops,
    sums,
    acc,
    mstat,
    lstat,
    seq_out,
    seq_in,
    seq_stat,
    seq_stat_in,
    side_out,
    side_in,
    stat_out,
    stat_in,
    own_acc,
    own_m,
    own_l,
    ids,
    hand,
    outgoing,
    kown,
    gain_wide,
    turn,
    hot,
    in_sem,
    key_sem,
    rs_send,
    rs_recv,
    seq_send,
    seq_recv,
    side_send,
    side_recv,
    hand_send,
    hand_recv,
    a2a_send,
    a2a_recv,
    share_send,
    share_recv,
    ready,
):
    side = lax.axis_index("side")
    owner = lax.axis_index("owner")
    seq = lax.axis_index("seq")
    quarter = side * 2 + seq
    y = owner % 2
    pair = owner // 2
    MESH = pl.DeviceIdType.MESH

    def flip(a, mask):
        out = a
        bit = 1
        while bit <= mask:
            if mask & bit:
                out = out + bit * (1 - 2 * ((a // bit) % 2))
            bit *= 2
        return out

    seq_peer = (side, owner, 1 - seq)
    side_peer = (1 - side, owner, seq)
    rs_peers = [(side, flip(owner, mask), seq) for mask in RING_MASKS + (1,)]

    def a2a_target(i):
        k = i % 16
        there = (pair + k) % 16
        to_y = (y + seq) % 2
        to_side = (side + i // 16) % 2
        return (to_side, there * 2 + to_y, 1 - seq), there

    barrier = pltpu.get_barrier_semaphore()
    for peer in rs_peers + [seq_peer, side_peer]:
        pl.semaphore_signal(barrier, inc=1, device_id=peer, device_id_type=MESH)


    hid_copy = pltpu.make_async_copy(hid_hbm, hid, in_sem.at[0])
    w_copy = pltpu.make_async_copy(w_hbm, w, in_sem.at[1])
    q_copy = pltpu.make_async_copy(query_hbm, qraw, in_sem.at[2])

    def key_copy(r):
        return pltpu.make_async_copy(
            cache_hbm.at[r], keys.at[r % 2, pl.ds(0, WIDTH)], key_sem.at[r % 2]
        )

    w_copy.start()
    hid_copy.start()

    dest = dest_ref[:, pl.ds(pl.multiple_of(owner * 128, 128), 128)].astype(F32)
    dest_lane = jnp.broadcast_to(dest, (128, 128))
    dest_sub = dest_lane.T
    order_sub = jnp.broadcast_to(order_ref[...].astype(F32), (128, 128)).T
    sub = lax.broadcasted_iota(jnp.int32, (128, 128), 0)
    lane = lax.broadcasted_iota(jnp.int32, (128, 128), 1)
    slot = jnp.sum(jnp.where(order_sub == dest_lane, sub, 0), axis=0, keepdims=True)
    rank = jnp.sum(
        jnp.where((dest_sub == dest_lane) & (sub < lane), 1, 0), axis=0, keepdims=True
    )
    row_id = (slot // 4) * 16 + (slot % 4) * 4 + seq * 2 + rank
    ids[0] = jnp.broadcast_to(row_id, (8, 128))

    w_copy.wait()
    wt[...] = w[...].T
    hid_copy.wait()
    q_copy.start()
    key_copy(0).start()
    key_copy(1).start()

    def project(flips):
        at = flip(owner, flips_mask(flips)) // 2
        block = jnp.dot(
            wt[...],
            hid[:, pl.ds(pl.multiple_of(at * 256, 256), 256)],
            preferred_element_type=F32,
        ).astype(BF16)
        for half in range(2):
            rel = (half + y) % 2
            for p in range(4):
                part[p, piece_slot(p, flips, rel)] = block[
                    p * PIECE : (p + 1) * PIECE, half * 128 : (half + 1) * 128
                ]

    starts = (0, 16, 24, 28, 30)

    def rs_copy(stage, p, sub_part):
        held = 32 >> stage
        if stage == 4:
            lo, n = 1, 1
            peer = rs_peers[(p + 3) % 4 if p == EARLY_Y else 4]
        else:
            n = held // 4
            lo = held // 2 + (n if sub_part == 0 else 0)
            peer = rs_peers[4 if stage == 3 and p == EARLY_Y else (p + stage) % 4]
        index = (stage * 2 + sub_part) * 4 + p
        return pltpu.make_async_remote_copy(
            part.at[p, pl.ds(lo, n)],
            landed.at[p, pl.ds(starts[stage] + lo - held // 2, n)],
            rs_send.at[index],
            rs_recv.at[index],
            peer,
            device_id_type=MESH,
        )

    def rs_part(stage, sub_part):
        for p in range(4):
            rs_copy(stage, p, sub_part).start()

    def rs_take(stage, sub_part, p):
        held = 32 >> stage
        n = held // 4
        lo = n if sub_part == 0 else 0
        rs_copy(stage, p, sub_part).wait_recv()

        def add(j, _):
            part[p, lo + j] = part[p, lo + j] + landed[p, starts[stage] + lo + j]
            return 0

        lax.fori_loop(0, n, add, 0)

    def rs_first(stage):
        for p in range(4):
            rs_take(stage, 0, p)
            for sub_part in range(2 if stage < 3 else 1):
                rs_copy(stage + 1, p, sub_part).start()

    def rs_second(stage):
        for p in range(4):
            rs_take(stage, 1, p)

    for flips in (15, 7, 11, 13, 14, 3, 6, 12, 9):
        project(flips)
    pl.semaphore_wait(barrier, 7)
    rs_part(0, 0)
    for flips in (5, 10, 1, 2, 4, 8, 0):
        project(flips)
    rs_part(0, 1)
    id_copy = pltpu.make_async_remote_copy(
        ids.at[0], ids.at[1], hand_send.at[0], hand_recv.at[0], seq_peer, device_id_type=MESH
    )
    id_copy.start()

    kown[NEW : NEW + 128, :] = jnp.zeros((128, PAD), BF16)
    new_all = jnp.concatenate([new_ref[u].astype(F32) for u in range(4)], axis=0)
    kown[NEW : NEW + 16, 0:WIDTH] = new_all.astype(BF16)
    marks = jnp.where(
        lax.broadcasted_iota(jnp.int32, (PAD - WIDTH, 128), 0) == 0, -1.0, 0.0
    ).astype(BF16)
    for c in range(2):
        hand[c, WIDTH:PAD, :] = marks

    q_copy.wait()

    def queries_in(r):
        lead = jnp.where(
            lax.broadcasted_iota(jnp.int32, (128, EXT - WIDTH), 1) == 0, masked_score, 0.0
        ).astype(BF16)
        for s in range(4):
            rows = qraw[s, r].T
            for hq in range(4):
                rel_seq = (hq + seq) % 2
                rel_side = (hq // 2 + side) % 2
                at = pl.multiple_of((rel_seq * 2 + rel_side) * 128 + s * 32, 32)
                qx[r % 2, pl.ds(at, 32), 0:WIDTH] = rows[hq * 32 : (hq + 1) * 32]
        for s in range(4):
            qx[r % 2, s * 128 : (s + 1) * 128, WIDTH:EXT] = lead
        qown[r * 128 : (r + 1) * 128, :] = qx[r % 2, 0:128, :]

    def dead_row(r):
        place = lax.broadcasted_iota(jnp.int32, (EXT - WIDTH, KEYS), 1) + quarter * KEYS
        first = lax.broadcasted_iota(jnp.int32, (EXT - WIDTH, KEYS), 0) == 0
        keys[r % 2, WIDTH:EXT, :] = jnp.where(
            (place >= lens_ref[r]) & first, 1.0, 0.0
        ).astype(BF16)

    def seq_copies(r):
        return [
            pltpu.make_async_remote_copy(
                src.at[r],
                dst.at[r],
                seq_send.at[r * 2 + i],
                seq_recv.at[r * 2 + i],
                seq_peer,
                device_id_type=MESH,
            )
            for i, (src, dst) in enumerate(((seq_out, seq_in), (seq_stat, seq_stat_in)))
        ]

    def compact(m, total):
        eight = lax.broadcasted_iota(jnp.int32, (8, 128), 0)
        return jnp.where(eight < 4, m.T[0:8], total.T[0:8])

    def spread(tile):
        return (
            jnp.broadcast_to(tile[0:1], (128, 128)).T,
            jnp.broadcast_to(tile[4:5], (128, 128)).T,
        )

    def side_copies(r):
        return [
            pltpu.make_async_remote_copy(
                src.at[r],
                dst.at[r],
                side_send.at[r * 2 + i],
                side_recv.at[r * 2 + i],
                side_peer,
                device_id_type=MESH,
            )
            for i, (src, dst) in enumerate(((side_out, side_in), (stat_out, stat_in)))
        ]

    def seq_start(r):
        total = jnp.sum(sums[...], axis=1, keepdims=True)
        lstat[r] = jnp.broadcast_to(total, (ROWS, 128))
        for half in range(2):
            rows = pl.ds(256 + half * 128, 128)
            seq_out[r, half] = acc[r, rows].astype(BF16)
            seq_stat[r, half] = compact(mstat[r, rows], lstat[r, rows])
        for copy in seq_copies(r):
            copy.start()

    def wide(x):
        return jnp.concatenate([x] * 4, axis=1)

    def seq_join(r):
        for copy in seq_copies(r):
            copy.wait_recv()
        for half in (1, 0):
            rows = pl.ds(half * 128, 128)
            m_a, l_a = mstat[r, rows], lstat[r, rows]
            m_b, l_b = spread(seq_stat_in[r, half])
            top = jnp.maximum(m_a, m_b)
            e_a, e_b = jnp.exp2(m_a - top), jnp.exp2(m_b - top)
            total = l_a * e_a + l_b * e_b
            joined = acc[r, rows] * wide(e_a) + seq_in[r, half].astype(F32) * wide(e_b)
            if half == 1:
                side_out[r] = joined.astype(BF16)
                stat_out[r] = compact(top, total)
                for copy in side_copies(r):
                    copy.start()
            else:
                own_acc[r] = joined
                own_m[r] = top
                own_l[r] = total

    def side_join(r):
        for copy in side_copies(r):
            copy.wait_recv()
        m_a = own_m[r]
        m_b, l_b = spread(stat_in[r])
        top = jnp.maximum(m_a, m_b)
        e_a, e_b = jnp.exp2(m_a - top), jnp.exp2(m_b - top)
        own_l[r] = own_l[r] * e_a + l_b * e_b
        own_m[r] = top
        own_acc[r] = own_acc[r] * wide(e_a) + side_in[r].astype(F32) * wide(e_b)

    def before_handing():
        gain_wide[...] = jnp.broadcast_to(gain_ref[...], (128, LATENT)).T
        token = (
            quarter * 4096 + owner * 128 + lax.broadcasted_iota(jnp.int32, (32, 128), 1)
        )
        began = jnp.zeros((32, 128), jnp.int32)
        start = jnp.int32(0)
        for p in range(4):
            began = jnp.maximum(began, jnp.where(start <= token, start, 0))
            start = start + plens_ref[p]
        which = lax.broadcasted_iota(jnp.int32, (32, 128), 0)
        frequency = jnp.ones((32, 128), F32)
        for i in range(1, 32):
            frequency = jnp.where(which == i, rope_theta ** (-i / 32), frequency)
        angle = (token - began).astype(F32) * frequency
        turn[0] = jnp.cos(angle)
        turn[1] = jnp.sin(angle)

    def places():
        id_copy.wait_recv()
        to_y = (y + seq) % 2
        for c in range(2):
            group = ids[c, 0:1] // 16
            place = jnp.where(group % 2 == to_y, (group // 2) * 16 + ids[c, 0:1] % 16, -1)
            hot[c] = jnp.where(
                lax.broadcasted_iota(jnp.int32, (256, 128), 0) == place, 1.0, 0.0
            ).astype(BF16)

    def handed():
        rows = []
        for p in range(4):
            rs_copy(4, p, 0).wait_recv()
            rows.append(part[p, 0].astype(F32) + landed[p, starts[4]].astype(F32))
        row = jnp.concatenate(rows, axis=0)
        latent = row[0:LATENT]
        mean = jnp.sum(latent * latent, axis=0, keepdims=True) * (1.0 / LATENT)
        hand[0, 0:LATENT, :] = (latent * lax.rsqrt(mean + norm_eps) * gain_wide[...]).astype(BF16)
        cosine, sine = turn[0], turn[1]
        b, c = row[LATENT : LATENT + 32], row[LATENT + 32 : WIDTH]
        hand[0, LATENT : LATENT + 32, :] = (b * cosine - c * sine).astype(BF16)
        hand[0, LATENT + 32 : WIDTH, :] = (b * sine + c * cosine).astype(BF16)

    hand_copy = pltpu.make_async_remote_copy(
        hand.at[0, pl.ds(0, WIDTH)],
        hand.at[1, pl.ds(0, WIDTH)],
        hand_send.at[1],
        hand_recv.at[1],
        seq_peer,
        device_id_type=MESH,
    )

    def pack_rows():
        packed = jnp.where(lax.broadcasted_iota(jnp.int32, (256, PAD), 1) == WIDTH, 1.0, 0.0)
        for c in range(2):
            packed = packed + lax.dot_general(
                hot[c], hand[c], (((1,), (1,)), ((), ())), preferred_element_type=F32
            )
        outgoing[...] = packed.astype(BF16)

    def a2a_copy(i):
        device, there = a2a_target(i)
        return pltpu.make_async_remote_copy(
            outgoing.at[pl.ds(pl.multiple_of(there * 16, 16), 16)],
            kown.at[pl.ds(pl.multiple_of(i * 16 + (i // 16) * (OTHER - 256), 16), 16)],
            a2a_send.at[i],
            a2a_recv.at[i],
            device,
            device_id_type=MESH,
        )

    def share_copy(i):
        return pltpu.make_async_remote_copy(
            kown.at[pl.ds(i * OTHER, 256)],
            kown.at[pl.ds(i * OTHER + 256, 256)],
            share_send.at[i],
            share_recv.at[i],
            seq_peer,
            device_id_type=MESH,
        )

    def own_part(lo, n):
        part_scores = lax.dot_general(
            qown[...],
            kown[lo : lo + n, 0:EXT],
            (((1,), (1,)), ((), ())),
            preferred_element_type=F32,
        )
        column = lax.broadcasted_iota(jnp.int32, (1, 512), 1)
        new_column = lax.broadcasted_iota(jnp.int32, (128, 128), 1)
        new_step = lax.broadcasted_iota(jnp.int32, (128, 128), 0) // 32
        for r in range(REQ):
            rows = part_scores[r * 128 : (r + 1) * 128]
            masked = jnp.where((column // 4) % 4 == r, rows[:, 0:512], masked_score)
            if n > 512:
                live = (new_column < 16) & (new_column % 4 == r) & (new_column // 4 <= new_step)
                late = jnp.where(live, rows[:, 512:n], masked_score)
                masked = jnp.concatenate([masked, late], axis=1)
            masked = masked * score_scale
            m_a = own_m[r]
            top = jnp.maximum(m_a, jnp.max(masked, axis=1, keepdims=True))
            e_a = jnp.exp2(m_a - top)
            weights = jnp.exp2(masked - top[:, 0:1])
            own_m[r] = top
            own_l[r] = own_l[r] * e_a + jnp.sum(weights, axis=1, keepdims=True)
            own_acc[r] = own_acc[r] * wide(e_a) + jnp.dot(
                weights.astype(BF16), kown[lo : lo + n, 0:LATENT], preferred_element_type=F32
            )

    def loop(lo, hi, f):
        def step(i, _):
            f(i)
            return 0

        lax.fori_loop(lo, hi, step, 0)

    hooks = {
        (0, 2): [before_handing],
        (0, 3): [places],
        (1, 0): [lambda: rs_first(0)],
        (1, 3): [lambda: rs_second(0), lambda: seq_join(0)],
        (2, 0): [lambda: rs_first(1)],
        (2, 1): [lambda: side_join(0)],
        (2, 2): [lambda: rs_second(1)],
        (2, 3): [lambda: rs_first(2), lambda: seq_join(1)],
        (3, 0): [lambda: rs_second(2)],
        (3, 1): [lambda: rs_first(3)],
        (3, 2): [lambda: rs_second(3), lambda: seq_join(2), lambda: side_join(1)],
    }

    def fresh_scores(r, c):
        step = KEYS // CHUNKS[r]
        at = pl.ds(c * step, step)
        fresh = jnp.dot(qx[r % 2], keys[r % 2, :, at], preferred_element_type=F32)
        scores[c % 2, :, 0:step] = fresh
        tops[c % 2] = functools.reduce(
            jnp.maximum, [fresh[:, j * 128 : (j + 1) * 128] for j in range(step // 128)]
        )

    def weigh(r, c):
        step = KEYS // CHUNKS[r]
        at = pl.ds(c * step, step)
        before = mstat[r]
        m = jnp.maximum(before, jnp.max(tops[c % 2], axis=1, keepdims=True) * score_scale)
        mstat[r] = m
        fade = jnp.exp2(before - m)
        ready = scores[c % 2, :, 0:step]
        weights = [
            jnp.exp2(ready[:, j * 128 : (j + 1) * 128] * score_scale - m)
            for j in range(step // 128)
        ]
        sums[...] = sums[...] * fade + functools.reduce(jnp.add, weights)
        acc[r] = acc[r] * wide(fade) + lax.dot_general(
            jnp.concatenate(weights, axis=1).astype(BF16),
            keys[r % 2, 0:LATENT, at],
            (((1,), (1,)), ((), ())),
            preferred_element_type=F32,
        )

    def chunks(r, first, last):
        for c in range(first, last):
            for act in hooks.get((r, c), ()):
                act()
            fresh_scores(r, c)
            weigh(r, c - 1)

    for r in range(REQ):
        queries_in(r)
        dead_row(r)
        key_copy(r).wait()
        for act in hooks.get((r, 0), ()):
            act()
        fresh_scores(r, 0)
        if r > 0:
            weigh(r - 1, CHUNKS[r - 1] - 1)
            seq_start(r - 1)
            if r + 1 < REQ:
                key_copy(r + 1).start()
        mstat[r] = jnp.full((ROWS, 128), -3e38, F32)
        sums[...] = jnp.zeros((ROWS, 128), F32)
        acc[r] = jnp.zeros((ROWS, LATENT), F32)
        chunks(r, 1, CHUNKS[r] if r + 1 < REQ else CUTS[0])

    handed()
    hand_copy.start()
    chunks(REQ - 1, CUTS[0], CUTS[1])
    hand_copy.wait_recv()
    pl.semaphore_signal(ready, inc=1, device_id=side_peer, device_id_type=MESH)
    pack_rows()
    loop(0, 16, lambda i: a2a_copy(i).start())
    pl.semaphore_wait(ready, 1)
    loop(16, 32, lambda i: a2a_copy(i).start())
    chunks(REQ - 1, CUTS[1], CHUNKS[REQ - 1])
    weigh(REQ - 1, CHUNKS[REQ - 1] - 1)
    seq_start(3)
    side_join(2)
    loop(0, 16, lambda i: a2a_copy(i).wait_recv())
    share_copy(0).start()
    seq_join(3)
    share_copy(0).wait_recv()
    own_part(0, OTHER)
    loop(16, 32, lambda i: a2a_copy(i).wait_recv())
    share_copy(1).start()
    side_join(3)
    share_copy(1).wait_recv()
    own_part(OTHER, 512)
    for r in range(REQ):
        result = own_acc[r] / wide(own_l[r])
        for s in range(4):
            out_ref[s, r] = result[s * 32 : (s + 1) * 32].astype(BF16)

    for stage in range(5):
        for sub_part in range(2 if stage < 4 else 1):
            for p in range(4):
                rs_copy(stage, p, sub_part).wait_send()
    for r in range(REQ):
        for copy in seq_copies(r) + side_copies(r):
            copy.wait_send()
    id_copy.wait_send()
    hand_copy.wait_send()
    loop(0, 32, lambda i: a2a_copy(i).wait_send())
    share_copy(0).wait_send()
    share_copy(1).wait_send()


def on_device(
    prompt_hidden,
    latent_weight,
    kv_gain,
    prompt_lengths,
    destination,
    request_order,
    cache,
    cache_lengths,
    queries,
    new_rows,
):
    smem = pl.BlockSpec(memory_space=pltpu.SMEM)
    vmem = pl.BlockSpec(memory_space=pltpu.VMEM)
    hbm = pl.BlockSpec(memory_space=pl.ANY)
    dma = pltpu.SemaphoreType.DMA
    return pl.pallas_call(
        kernel,
        out_shape=jax.ShapeDtypeStruct((4, 4, 32, LATENT), BF16),
        in_specs=[smem, smem, hbm, hbm, vmem, vmem, vmem, hbm, hbm, vmem],
        out_specs=vmem,
        scratch_shapes=[
            pltpu.VMEM((224, 4096), BF16),
            pltpu.VMEM((224, WIDTH), BF16),
            pltpu.VMEM((WIDTH, 224), BF16),
            pltpu.VMEM((4, 32, PIECE, 128), BF16),
            pltpu.VMEM((4, 31, PIECE, 128), BF16),
            pltpu.VMEM((2, EXT, KEYS), BF16),
            pltpu.VMEM((4, 4, WIDTH, HEADS), BF16),
            pltpu.VMEM((2, ROWS, EXT), BF16),
            pltpu.VMEM((ROWS, EXT), BF16),
            pltpu.VMEM((2, ROWS, KEYS // 4), F32),
            pltpu.VMEM((2, ROWS, 128), F32),
            pltpu.VMEM((ROWS, 128), F32),
            pltpu.VMEM((REQ, ROWS, LATENT), F32),
            pltpu.VMEM((REQ, ROWS, 128), F32),
            pltpu.VMEM((REQ, ROWS, 128), F32),
            pltpu.VMEM((REQ, 2, 128, LATENT), BF16),
            pltpu.VMEM((REQ, 2, 128, LATENT), BF16),
            pltpu.VMEM((REQ, 2, 8, 128), F32),
            pltpu.VMEM((REQ, 2, 8, 128), F32),
            pltpu.VMEM((REQ, 128, LATENT), BF16),
            pltpu.VMEM((REQ, 128, LATENT), BF16),
            pltpu.VMEM((REQ, 8, 128), F32),
            pltpu.VMEM((REQ, 8, 128), F32),
            pltpu.VMEM((REQ, 128, LATENT), F32),
            pltpu.VMEM((REQ, 128, 128), F32),
            pltpu.VMEM((REQ, 128, 128), F32),
            pltpu.VMEM((2, 8, 128), jnp.int32),
            pltpu.VMEM((2, PAD, 128), BF16),
            pltpu.VMEM((256, PAD), BF16),
            pltpu.VMEM((1152, PAD), BF16),
            pltpu.VMEM((LATENT, 128), F32),
            pltpu.VMEM((2, 32, 128), F32),
            pltpu.VMEM((2, 256, 128), BF16),
            dma((3,)),
            dma((2,)),
            dma((36,)),
            dma((36,)),
            dma((8,)),
            dma((8,)),
            dma((8,)),
            dma((8,)),
            dma((2,)),
            dma((2,)),
            dma((32,)),
            dma((32,)),
            dma((2,)),
            dma((2,)),
            pltpu.SemaphoreType.REGULAR,
        ],
        compiler_params=pltpu.CompilerParams(
            collective_id=0, has_side_effects=True, vmem_limit_bytes=62 << 20
        ),
        cost_estimate=pl.CostEstimate(
            flops=20_000_000_000, bytes_accessed=24_000_000, transcendentals=8_400_000
        ),
    )(
        cache_lengths,
        prompt_lengths,
        prompt_hidden.T,
        latent_weight,
        kv_gain.reshape(1, LATENT),
        destination.T,
        request_order.reshape(1, 128),
        jnp.transpose(cache, (0, 2, 1)),
        jnp.transpose(queries, (0, 1, 3, 2)),
        new_rows,
    )


def solution(mesh):
    return jax.shard_map(
        on_device,
        mesh=mesh,
        in_specs=(
            P(("side", "seq"), "owner"),
            P("owner", None),
            P(),
            P(),
            P(("side", "seq"), None),
            P(),
            P("owner", ("side", "seq"), None),
            P("owner"),
            P(None, "owner", None, None),
            P(None, "owner", None),
        ),
        out_specs=P(None, "owner", ("side", "seq"), None),
        check_vma=False,
    )
```
